32 devices in a mesh: groups: 2 (over x), inst: 8 (over z, y), space: 2 (over core).
Axes of the slice: x: 2, y: 2, z: 4, core: 2. Of those that a mesh axis runs over, the one named last changes fastest.
Arguments:
- flow: float32 [16, 5, 64, 1024], P(('groups', 'inst'), None, 'space'), parts along dimension 0, may hold values from -4 to 15, as said below
- grid_velocity: float32 [16, 2, 64, 1024], P(('groups', 'inst'), None, 'space'), parts along dimension 0, may hold values from -0.4 to 0.4
- cell_volume: float32 [64, 1024], P('space'), may hold values from 0.5 to 2
Outputs:
- flow_next: float32 [16, 5, 64, 1024], P(('groups', 'inst'), None, 'space'), parts along dimension 0
- mean_flow: float32 [10, 64, 1024], P('groups', 'space', 'inst'), parts along dimension 0
The draws below stay inside these ranges and needn't reach their ends.
There are 2 independent parts, one for each index of `groups`. The reference program is written for one: setup_inputs(seed, part) draws one part's arguments, and reference() takes and returns one part's arrays. A program takes and returns all parts, laid end to end along the dimension named above; an argument that names none is the same for every part. Nothing has to cross between parts.
Inputs may be any that keep to these rules, and one draw needn't show every extreme that they name: `flow`: each cell's state has density and implied pressure between 0.3 and 3, and speeds of at most 1.2 along each direction.
All inputs are finite; a program needn't handle non-finite values.
Results may differ from the reference program's by a relative error of at most 0.00005.
Values sent between devices are 32-bit elements; how exact they have to be, the bound alone decides.
A program may use at most 128 MiB of HBM per device.

```python
import math
import jax
import jax.numpy as jnp
import numpy as np
from jax import lax

NY = 1024
INSTANCES = 8
NX = 64


def draw_flow(key, part):
    subkeys = jax.random.split(key, 3)
    grid_shape = (INSTANCES, NX, NY)
    density = jnp.exp(jax.random.uniform(subkeys[0], grid_shape, jnp.float32, math.log(0.5), math.log(2.0)))
    velocity = jnp.clip(0.4 * jax.random.normal(subkeys[1], (INSTANCES, 3, NX, NY), jnp.float32), -1.2, 1.2)
    pressure = jnp.exp(jax.random.uniform(subkeys[2], grid_shape, jnp.float32, math.log(0.5), math.log(2.0)))
    momentum = density[:, None] * velocity
    energy = pressure / 0.4 + 0.5 * density * jnp.sum(velocity * velocity, axis=1)
    return jnp.concatenate([density[:, None], momentum, energy[:, None]], axis=1)


def level_of(stream_key, dims, pieces, low, high):
    def one(position, parts):
        steps = jax.random.uniform(jax.random.fold_in(jax.random.fold_in(stream_key, 6), position), (parts,), jnp.float32, low / len(pieces), high / len(pieces))
        return jnp.repeat(jnp.exp(steps), dims[position] // parts).reshape((-1,) + (1,) * (len(dims) - position - 1))

    level = one(*pieces[0])
    for cut in pieces[1:]:
        level = level * one(*cut)
    return level


def setup_inputs(seed: int = 0, part: int = 0) -> dict:
    splits = jax.random.split(jax.random.key(seed), 4)
    own_keys = jax.random.split(jax.random.fold_in(splits[3], part), 4)
    flow = draw_flow(jax.random.fold_in(jax.random.fold_in(splits[3], part), 71), part)
    grid_velocity = jnp.clip(jax.random.uniform(own_keys[1], (INSTANCES, 2, NX, NY), jnp.float32, -0.4, 0.4) * level_of(own_keys[1], (INSTANCES, 2, NX, NY), ((0, 8), (2, 2)), -0.4, 0.0), -0.4, 0.4)
    cell_volume = jnp.clip(jnp.exp(math.log(2.0) - 1.3862944 * jax.random.uniform(splits[2], (NX, NY), jnp.float32) ** level_of(splits[2], (NX, NY), ((0, 2),), -0.2, 0.2)), 0.5, 2.0)
    return {"flow": flow, "grid_velocity": grid_velocity, "cell_volume": cell_volume}


gamma_ratio = 1.4
courant_number = 1.5
section_weight = 0.5

def coefficient(offsets, inst_count):
    parity = (offsets % 2).astype(jnp.float32)
    angle = math.pi / inst_count * offsets.astype(jnp.float32)
    safe_sine = jnp.where(offsets == 0, 1.0, jnp.sin(angle))
    value = (1.0 - 2.0 * parity) * (math.pi / inst_count) * jnp.cos(angle) / safe_sine
    return jnp.where(offsets == 0, 0.0, value)

def cell_state(state):
    density = state[:, 0]
    velocity = state[:, 1:4] / density[:, None]
    kinetic = 0.5 * lax.optimization_barrier(jnp.sum(state[:, 1:4] * velocity, axis=1))
    pressure = (gamma_ratio - 1.0) * (state[:, 4] - kinetic)
    sound = jnp.sqrt(gamma_ratio * pressure / density)
    return (velocity, pressure, sound)

def side_flux(state, face_speed, normal):
    velocity, pressure, sound = cell_state(state)
    normal_speed = velocity[:, normal]
    relative = normal_speed - face_speed
    unit_push = jnp.asarray(np.eye(5, dtype=np.float32)[1 + normal]).reshape(1, 5, 1, 1)
    unit_work = jnp.asarray(np.eye(5, dtype=np.float32)[4]).reshape(1, 5, 1, 1)
    flux = state * relative[:, None] + pressure[:, None] * unit_push + (pressure * normal_speed)[:, None] * unit_work
    return (flux, jnp.abs(relative) + sound)

def face_flux(left_state, right_state, left_grid, right_grid, normal):
    face_speed = 0.5 * (left_grid[:, normal] + right_grid[:, normal])
    flux_left, reach_left = side_flux(left_state, face_speed, normal)
    flux_right, reach_right = side_flux(right_state, face_speed, normal)
    reach = jnp.maximum(reach_left, reach_right)
    return 0.5 * (flux_left + flux_right) - 0.5 * reach[:, None] * (right_state - left_state)

def section_update(flow, grid_velocity, cell_volume, ext_state, ext_grid, derivative):
    flux_x = face_flux(ext_state[:, :, :-1], ext_state[:, :, 1:], ext_grid[:, :, :-1], ext_grid[:, :, 1:], 0)
    state_y = jnp.concatenate([flow[..., :1], flow, flow[..., -1:]], axis=3)
    grid_y = jnp.concatenate([grid_velocity[..., :1], grid_velocity, grid_velocity[..., -1:]], axis=3)
    flux_y = face_flux(state_y[..., :-1], state_y[..., 1:], grid_y[..., :-1], grid_y[..., 1:], 1)
    divergence = (flux_x[:, :, 1:] - flux_x[:, :, :-1] + flux_y[..., 1:] - flux_y[..., :-1]) / cell_volume
    residual = derivative + divergence
    velocity, pressure, sound = cell_state(flow)
    reach_sum = jnp.abs(velocity[:, 0] - grid_velocity[:, 0]) + jnp.abs(velocity[:, 1] - grid_velocity[:, 1]) + 2.0 * sound
    pseudo_step = courant_number * cell_volume / (reach_sum + math.pi * cell_volume)
    return flow - section_weight * pseudo_step[:, None] * residual

def reference(flow, grid_velocity, cell_volume):
    inst_count = flow.shape[0]
    indices = jnp.arange(inst_count, dtype=jnp.int32)
    matrix = coefficient((indices[:, None] - indices[None, :]) % inst_count, inst_count)
    derivative = jnp.einsum('nj,jvxy->nvxy', matrix, flow, precision=lax.Precision.HIGHEST)
    mean_flow = lax.optimization_barrier(jnp.sum(flow, axis=0)) / inst_count
    ext_state = jnp.concatenate([flow[:, :, -1:], flow, flow[:, :, :1]], axis=2)
    ext_grid = jnp.concatenate([grid_velocity[:, :, -1:], grid_velocity, grid_velocity[:, :, :1]], axis=2)
    flow_next = section_update(flow, grid_velocity, cell_volume, ext_state, ext_grid, derivative)
    return (flow_next, mean_flow)
```

```python
import functools
import math

import jax
import jax.numpy as jnp
import numpy as np
from jax import lax
from jax.experimental import pallas as pl
from jax.experimental.pallas import tpu as pltpu
from jax.sharding import PartitionSpec as P

gamma_ratio = 1.4
courant_number = 1.5
section_weight = 0.5


def extended_2(x, sides, width):
    for axis, dim in sides:
        devices, length = (lax.axis_size(axis), x.shape[dim])
        up = [(i, (i + 1) % devices) for i in range(devices)]
        down = [(j, i) for i, j in up]
        last = lax.slice_in_dim(x, length - width, length, axis=dim)
        leading = lax.slice_in_dim(x, 0, width, axis=dim)
        before = lax.ppermute(last, axis, up)
        after = lax.ppermute(leading, axis, down)
        x = jnp.concatenate([before, x, after], axis=dim)
    return x


def coefficient(offsets, inst_count):
    parity = (offsets % 2).astype(jnp.float32)
    angle = math.pi / inst_count * offsets.astype(jnp.float32)
    safe_sine = jnp.where(offsets == 0, 1.0, jnp.sin(angle))
    value = (1.0 - 2.0 * parity) * (math.pi / inst_count) * jnp.cos(angle) / safe_sine
    return jnp.where(offsets == 0, 0.0, value)


def cell_state(state):
    density = state[:, 0]
    velocity = state[:, 1:4] / density[:, None]
    kinetic = 0.5 * jnp.sum(state[:, 1:4] * velocity, axis=1)
    pressure = (gamma_ratio - 1.0) * (state[:, 4] - kinetic)
    sound = jnp.sqrt(gamma_ratio * pressure / density)
    return (velocity, pressure, sound)


def side_flux(state, face_speed, normal):
    velocity, pressure, sound = cell_state(state)
    normal_speed = velocity[:, normal]
    relative = normal_speed - face_speed
    unit_push = jnp.asarray(np.eye(5, dtype=np.float32)[1 + normal]).reshape(1, 5, 1, 1)
    unit_work = jnp.asarray(np.eye(5, dtype=np.float32)[4]).reshape(1, 5, 1, 1)
    flux = (
        state * relative[:, None]
        + pressure[:, None] * unit_push
        + (pressure * normal_speed)[:, None] * unit_work
    )
    return (flux, jnp.abs(relative) + sound)


def face_flux(left_state, right_state, left_grid, right_grid, normal):
    face_speed = 0.5 * (left_grid[:, normal] + right_grid[:, normal])
    flux_left, reach_left = side_flux(left_state, face_speed, normal)
    flux_right, reach_right = side_flux(right_state, face_speed, normal)
    reach = jnp.maximum(reach_left, reach_right)
    return 0.5 * (flux_left + flux_right) - 0.5 * reach[:, None] * (right_state - left_state)


def section_update(flow, grid_velocity, cell_volume, ext_state, ext_grid, derivative):
    flux_x = face_flux(
        ext_state[:, :, :-1], ext_state[:, :, 1:], ext_grid[:, :, :-1], ext_grid[:, :, 1:], 0
    )
    state_y = jnp.concatenate([flow[..., :1], flow, flow[..., -1:]], axis=3)
    grid_y = jnp.concatenate(
        [grid_velocity[..., :1], grid_velocity, grid_velocity[..., -1:]], axis=3
    )
    flux_y = face_flux(state_y[..., :-1], state_y[..., 1:], grid_y[..., :-1], grid_y[..., 1:], 1)
    divergence = (
        flux_x[:, :, 1:] - flux_x[:, :, :-1] + flux_y[..., 1:] - flux_y[..., :-1]
    ) / cell_volume
    residual = derivative + divergence
    velocity, pressure, sound = cell_state(flow)
    reach_sum = (
        jnp.abs(velocity[:, 0] - grid_velocity[:, 0])
        + jnp.abs(velocity[:, 1] - grid_velocity[:, 1])
        + 2.0 * sound
    )
    pseudo_step = courant_number * cell_volume / (reach_sum + math.pi * cell_volume)
    return flow - section_weight * pseudo_step[:, None] * residual


def body(flow, grid_velocity, cell_volume):
    inst_count = lax.axis_size("inst")
    own_index = lax.axis_index("inst")
    packed = jnp.concatenate([flow, grid_velocity], axis=1)
    extended = extended_2(packed, (("space", 2),), 1)
    ext_state = extended[:, :5]
    ext_grid = extended[:, 5:]
    slices = lax.all_gather(flow, "inst", axis=0, tiled=True)
    positions = jnp.arange(slices.shape[0], dtype=jnp.int32)
    weights = coefficient((own_index - positions) % inst_count, inst_count)
    added = jnp.einsum("j,jvxy->vxy", weights, slices, precision=lax.Precision.HIGHEST)
    derivative = added[None]
    summed = jnp.sum(slices, axis=0, keepdims=True)
    slab_width = flow.shape[3] // inst_count
    mean_flow = (
        lax.dynamic_slice_in_dim(summed[0], own_index * slab_width, slab_width, 2) / inst_count
    )
    flow_next = section_update(flow, grid_velocity, cell_volume, ext_state, ext_grid, derivative)
    return (flow_next, mean_flow)


LANES = 128


def spectral_weight(offset, count):
    if offset == 0:
        return 0.0
    angle = math.pi * offset / count
    return (-1.0) ** offset * (math.pi / count) * math.cos(angle) / math.sin(angle)


def cell_terms(state):
    inverse = 1.0 / state[0]
    speeds = [state[k] * inverse for k in (1, 2, 3)]
    kinetic = 0.5 * (state[1] * speeds[0] + state[2] * speeds[1] + state[3] * speeds[2])
    pressure = (gamma_ratio - 1.0) * (state[4] - kinetic)
    sound = jnp.sqrt(gamma_ratio * pressure * inverse)
    return speeds[0], speeds[1], pressure, sound


def rusanov(left, right, normal):
    state_l, speed_l, pressure_l, sound_l, grid_l = left
    state_r, speed_r, pressure_r, sound_r, grid_r = right
    face_speed = 0.5 * (grid_l + grid_r)
    relative_l = speed_l - face_speed
    relative_r = speed_r - face_speed
    reach = jnp.maximum(jnp.abs(relative_l) + sound_l, jnp.abs(relative_r) + sound_r)
    weight_l = 0.5 * (relative_l + reach)
    weight_r = 0.5 * (relative_r - reach)
    flux = [a * weight_l + b * weight_r for a, b in zip(state_l, state_r)]
    flux[1 + normal] += 0.5 * (pressure_l + pressure_r)
    flux[4] += 0.5 * (pressure_l * speed_l + pressure_r * speed_r)
    return flux


def on_side(change, side):
    return ([change(x) for x in side[0]],) + tuple(change(x) for x in side[1:])


def section_kernel(
    n,
    flow_ref,
    grid_ref,
    volume_ref,
    next_ref,
    mean_ref,
    slabs,
    rates,
    returned,
    step_ref,
    edge_out,
    edge_in,
    edge_send,
    edge_recv,
    slab_send,
    slab_recv,
    rate_send,
    rate_recv,
):
    variables, rows, columns = flow_ref.shape
    width = columns // n
    me = lax.axis_index("inst")
    other = 1 - lax.axis_index("space")
    order = sorted(range(1, n), key=lambda s: abs(2 * s - n))

    def peer(offset):
        return lax.rem(me + (offset + n), n)

    def columns_of(offset):
        return pl.ds(pl.multiple_of(peer(offset) * width, width), width)

    barrier = pltpu.get_barrier_semaphore()
    for s in range(1, n):
        pl.semaphore_signal(barrier, inc=1, device_id={"inst": peer(s)})
    pl.semaphore_signal(barrier, inc=1, device_id={"space": other})
    for edge, row in ((0, rows - 1), (1, 0)):
        for v in range(variables):
            edge_out[edge, v : v + 1, :] = flow_ref[v, row : row + 1, :]
        for v in range(2):
            edge_out[edge, variables + v : variables + v + 1, :] = grid_ref[v, row : row + 1, :]
        edge_out[edge, variables + 2 : variables + 3, :] = jnp.zeros((1, columns), jnp.float32)
    pl.semaphore_wait(barrier, n)

    edges = pltpu.make_async_remote_copy(
        src_ref=edge_out,
        dst_ref=edge_in,
        send_sem=edge_send,
        recv_sem=edge_recv,
        device_id={"space": other},
    )
    edges.start()
    for c in range(variables):
        for s in order:
            pltpu.make_async_remote_copy(
                src_ref=flow_ref.at[c, :, columns_of(s)],
                dst_ref=slabs.at[c, s - 1],
                send_sem=slab_send,
                recv_sem=slab_recv.at[c],
                device_id={"inst": peer(s)},
            ).start()

    state = [flow_ref[v] for v in range(variables)]
    grid_0, grid_1, volume = grid_ref[0], grid_ref[1], volume_ref[...]
    speed_0, speed_1, pressure, sound = cell_terms(state)
    wave = jnp.abs(speed_0 - grid_0) + jnp.abs(speed_1 - grid_1) + 2.0 * sound
    push = (section_weight * courant_number) / (wave + math.pi * volume)
    step_ref[...] = push * volume

    lane = lax.broadcasted_iota(jnp.int32, (rows, columns), 1)
    own = (state, speed_1, pressure, sound, grid_1)
    left = on_side(lambda x: jnp.where(lane == 0, x, pltpu.roll(x, 1, 1)), own)
    flux = rusanov(left, own, 1)
    end = on_side(lambda x: x[:, columns - LANES :], own)
    last = rusanov(end, end, 1)
    lane_end = lane[:, columns - LANES :]
    for v in range(variables):
        upper = pltpu.roll(flux[v], columns - 1, 1)
        upper_end = jnp.where(lane_end == columns - 1, last[v], upper[:, columns - LANES :])
        upper = jnp.concatenate([upper[:, : columns - LANES], upper_end], axis=1)
        next_ref[v] = state[v] - push * (upper - flux[v])

    edges.wait_recv()

    def edge_side(edge):
        edge_state = [edge_in[edge, v : v + 1, :] for v in range(variables)]
        speed, _, edge_pressure, edge_sound = cell_terms(edge_state)
        grid = edge_in[edge, variables : variables + 1, :]
        return (edge_state, speed, edge_pressure, edge_sound, grid)

    above, below = edge_side(0), edge_side(1)
    row = lax.broadcasted_iota(jnp.int32, (rows, columns), 0)
    own = (state, speed_0, pressure, sound, grid_0)
    rolled = on_side(lambda x: pltpu.roll(x, 1, 0), own)
    first = lambda x, y: jnp.where(row == 0, y, x)
    left = (
        [first(x, y) for x, y in zip(rolled[0], above[0])],
    ) + tuple(first(x, y) for x, y in zip(rolled[1:], above[1:]))
    flux = rusanov(left, own, 0)
    last = rusanov(on_side(lambda x: x[rows - 1 : rows], own), below, 0)
    for v in range(variables):
        upper = jnp.where(row == rows - 1, last[v], pltpu.roll(flux[v], rows - 1, 0))
        next_ref[v] = next_ref[v] - push * (upper - flux[v])

    for c in range(variables):
        got = slabs.at[c]
        pltpu.make_async_remote_copy(
            src_ref=got,
            dst_ref=got,
            send_sem=slab_send,
            recv_sem=slab_recv.at[c],
            device_id={"inst": peer(1)},
        ).wait_recv()
        held = [flow_ref[c, :, columns_of(0)]] + [slabs[c, s - 1] for s in range(1, n)]
        mean_ref[c] = functools.reduce(jnp.add, held) * (1.0 / n)

        def rate(t):
            terms = [held[s] * spectral_weight((s - t) % n, n) for s in range(n) if s != t]
            return functools.reduce(jnp.add, terms)

        for t in order:
            rates[c, t - 1] = rate(t)
            pltpu.make_async_remote_copy(
                src_ref=rates.at[c, t - 1],
                dst_ref=returned.at[c, t - 1],
                send_sem=rate_send,
                recv_sem=rate_recv.at[c],
                device_id={"inst": peer(-t)},
            ).start()
        at = columns_of(0)
        next_ref[c, :, at] = next_ref[c, :, at] - step_ref[:, at] * rate(0)

    for c in range(variables):
        got = returned.at[c]
        pltpu.make_async_remote_copy(
            src_ref=got,
            dst_ref=got,
            send_sem=rate_send,
            recv_sem=rate_recv.at[c],
            device_id={"inst": peer(1)},
        ).wait_recv()
        for t in range(1, n):
            at = columns_of(t)
            next_ref[c, :, at] = next_ref[c, :, at] - step_ref[:, at] * returned[c, t - 1]

    edges.wait_send()
    for sent, sem in ((slabs, slab_send), (rates, rate_send)):
        pltpu.make_async_remote_copy(
            src_ref=sent,
            dst_ref=sent,
            send_sem=sem,
            recv_sem=edge_recv,
            device_id={"inst": peer(1)},
        ).wait_send()


def kernel_body(flow, grid_velocity, cell_volume):
    n = lax.axis_size("inst")
    variables, rows, columns = flow.shape[1:]
    width = columns // n
    f32 = jnp.float32
    exchanged = pltpu.VMEM((variables, n - 1, rows, width), f32)
    edge = pltpu.VMEM((2, variables + 3, columns), f32)
    dma = pltpu.SemaphoreType.DMA
    flow_next, mean_flow = pl.pallas_call(
        functools.partial(section_kernel, n),
        out_shape=(
            jax.ShapeDtypeStruct((variables, rows, columns), f32),
            jax.ShapeDtypeStruct((variables, rows, width), f32),
        ),
        in_specs=[pl.BlockSpec(memory_space=pltpu.VMEM)] * 3,
        out_specs=[pl.BlockSpec(memory_space=pltpu.VMEM)] * 2,
        scratch_shapes=[
            exchanged,
            exchanged,
            exchanged,
            pltpu.VMEM((rows, columns), f32),
            edge,
            edge,
            dma,
            dma,
            dma,
            dma((variables,)),
            dma,
            dma((variables,)),
        ],
        compiler_params=pltpu.CompilerParams(
            collective_id=0, has_side_effects=True, vmem_limit_bytes=32 * 1024 * 1024
        ),
        name="section",
    )(flow[0], grid_velocity[0], cell_volume)
    return flow_next[None], mean_flow


def solution(mesh):
    in_specs = (
        P(("groups", "inst"), None, "space", None),
        P(("groups", "inst"), None, "space", None),
        P("space", None),
    )
    out_specs = (P(("groups", "inst"), None, "space", None), P("groups", "space", "inst"))

    def local(flow, grid_velocity, cell_volume):
        whole_lanes = flow.shape[3] % (LANES * mesh.shape["inst"]) == 0
        whole_rows = flow.shape[2] % 8 == 0 and flow.shape[2] >= 8
        fits = mesh.shape["space"] == 2 and mesh.shape["inst"] > 1 and flow.shape[0] == 1
        chosen = kernel_body if whole_lanes and whole_rows and fits else body
        return chosen(flow, grid_velocity, cell_volume)

    return jax.shard_map(local, mesh=mesh, in_specs=in_specs, out_specs=out_specs, check_vma=False)
```

```python
import functools
import math

import jax
import jax.numpy as jnp
import numpy as np
from jax import lax
from jax.experimental import pallas as pl
from jax.experimental.pallas import tpu as pltpu
from jax.sharding import PartitionSpec as P

gamma_ratio = 1.4
courant_number = 1.5
section_weight = 0.5


def extended_2(x, sides, width):
    for axis, dim in sides:
        devices, length = (lax.axis_size(axis), x.shape[dim])
        up = [(i, (i + 1) % devices) for i in range(devices)]
        down = [(j, i) for i, j in up]
        last = lax.slice_in_dim(x, length - width, length, axis=dim)
        leading = lax.slice_in_dim(x, 0, width, axis=dim)
        before = lax.ppermute(last, axis, up)
        after = lax.ppermute(leading, axis, down)
        x = jnp.concatenate([before, x, after], axis=dim)
    return x


def coefficient(offsets, inst_count):
    parity = (offsets % 2).astype(jnp.float32)
    angle = math.pi / inst_count * offsets.astype(jnp.float32)
    safe_sine = jnp.where(offsets == 0, 1.0, jnp.sin(angle))
    value = (1.0 - 2.0 * parity) * (math.pi / inst_count) * jnp.cos(angle) / safe_sine
    return jnp.where(offsets == 0, 0.0, value)


def cell_state(state):
    density = state[:, 0]
    velocity = state[:, 1:4] / density[:, None]
    kinetic = 0.5 * jnp.sum(state[:, 1:4] * velocity, axis=1)
    pressure = (gamma_ratio - 1.0) * (state[:, 4] - kinetic)
    sound = jnp.sqrt(gamma_ratio * pressure / density)
    return (velocity, pressure, sound)


def side_flux(state, face_speed, normal):
    velocity, pressure, sound = cell_state(state)
    normal_speed = velocity[:, normal]
    relative = normal_speed - face_speed
    unit_push = jnp.asarray(np.eye(5, dtype=np.float32)[1 + normal]).reshape(1, 5, 1, 1)
    unit_work = jnp.asarray(np.eye(5, dtype=np.float32)[4]).reshape(1, 5, 1, 1)
    flux = (
        state * relative[:, None]
        + pressure[:, None] * unit_push
        + (pressure * normal_speed)[:, None] * unit_work
    )
    return (flux, jnp.abs(relative) + sound)


def face_flux(left_state, right_state, left_grid, right_grid, normal):
    face_speed = 0.5 * (left_grid[:, normal] + right_grid[:, normal])
    flux_left, reach_left = side_flux(left_state, face_speed, normal)
    flux_right, reach_right = side_flux(right_state, face_speed, normal)
    reach = jnp.maximum(reach_left, reach_right)
    return 0.5 * (flux_left + flux_right) - 0.5 * reach[:, None] * (right_state - left_state)


def section_update(flow, grid_velocity, cell_volume, ext_state, ext_grid, derivative):
    flux_x = face_flux(
        ext_state[:, :, :-1], ext_state[:, :, 1:], ext_grid[:, :, :-1], ext_grid[:, :, 1:], 0
    )
    state_y = jnp.concatenate([flow[..., :1], flow, flow[..., -1:]], axis=3)
    grid_y = jnp.concatenate(
        [grid_velocity[..., :1], grid_velocity, grid_velocity[..., -1:]], axis=3
    )
    flux_y = face_flux(state_y[..., :-1], state_y[..., 1:], grid_y[..., :-1], grid_y[..., 1:], 1)
    divergence = (
        flux_x[:, :, 1:] - flux_x[:, :, :-1] + flux_y[..., 1:] - flux_y[..., :-1]
    ) / cell_volume
    residual = derivative + divergence
    velocity, pressure, sound = cell_state(flow)
    reach_sum = (
        jnp.abs(velocity[:, 0] - grid_velocity[:, 0])
        + jnp.abs(velocity[:, 1] - grid_velocity[:, 1])
        + 2.0 * sound
    )
    pseudo_step = courant_number * cell_volume / (reach_sum + math.pi * cell_volume)
    return flow - section_weight * pseudo_step[:, None] * residual


def body(flow, grid_velocity, cell_volume):
    inst_count = lax.axis_size("inst")
    own_index = lax.axis_index("inst")
    packed = jnp.concatenate([flow, grid_velocity], axis=1)
    extended = extended_2(packed, (("space", 2),), 1)
    ext_state = extended[:, :5]
    ext_grid = extended[:, 5:]
    slices = lax.all_gather(flow, "inst", axis=0, tiled=True)
    positions = jnp.arange(slices.shape[0], dtype=jnp.int32)
    weights = coefficient((own_index - positions) % inst_count, inst_count)
    added = jnp.einsum("j,jvxy->vxy", weights, slices, precision=lax.Precision.HIGHEST)
    derivative = added[None]
    summed = jnp.sum(slices, axis=0, keepdims=True)
    slab_width = flow.shape[3] // inst_count
    mean_flow = (
        lax.dynamic_slice_in_dim(summed[0], own_index * slab_width, slab_width, 2) / inst_count
    )
    flow_next = section_update(flow, grid_velocity, cell_volume, ext_state, ext_grid, derivative)
    return (flow_next, mean_flow)


LANES = 128


def spectral_weight(offset, count):
    if offset == 0:
        return 0.0
    angle = math.pi * offset / count
    return (-1.0) ** offset * (math.pi / count) * math.cos(angle) / math.sin(angle)


def cell_terms(state):
    inverse = 1.0 / state[0]
    speeds = [state[k] * inverse for k in (1, 2, 3)]
    kinetic = 0.5 * (state[1] * speeds[0] + state[2] * speeds[1] + state[3] * speeds[2])
    pressure = (gamma_ratio - 1.0) * (state[4] - kinetic)
    sound = jnp.sqrt(gamma_ratio * pressure * inverse)
    return speeds[0], speeds[1], pressure, sound


def rusanov(left, right, normal):
    state_l, speed_l, pressure_l, sound_l, grid_l = left
    state_r, speed_r, pressure_r, sound_r, grid_r = right
    face_speed = 0.5 * (grid_l + grid_r)
    relative_l = speed_l - face_speed
    relative_r = speed_r - face_speed
    reach = jnp.maximum(jnp.abs(relative_l) + sound_l, jnp.abs(relative_r) + sound_r)
    weight_l = 0.5 * (relative_l + reach)
    weight_r = 0.5 * (relative_r - reach)
    flux = [a * weight_l + b * weight_r for a, b in zip(state_l, state_r)]
    flux[1 + normal] += 0.5 * (pressure_l + pressure_r)
    flux[4] += 0.5 * (pressure_l * speed_l + pressure_r * speed_r)
    return flux


def on_side(change, side):
    return ([change(x) for x in side[0]],) + tuple(change(x) for x in side[1:])


def section_kernel(
    n,
    flow_hbm,
    grid_hbm,
    volume_hbm,
    next_ref,
    mean_ref,
    flow_ref,
    grid_ref,
    volume_ref,
    slabs,
    rates,
    returned,
    step_ref,
    edge_out,
    edge_in,
    edge_send,
    edge_recv,
    slab_send,
    slab_recv,
    rate_send,
    rate_recv,
    load_sem,
):
    variables, rows, columns = flow_ref.shape
    width = columns // n
    me = lax.axis_index("inst")
    other = 1 - lax.axis_index("space")
    order = sorted(range(1, n), key=lambda s: abs(2 * s - n))

    def peer(offset):
        return lax.rem(me + (offset + n), n)

    def columns_of(offset):
        return pl.ds(pl.multiple_of(peer(offset) * width, width), width)

    loads = [
        pltpu.make_async_copy(source, target, load_sem.at[k])
        for k, (source, target) in enumerate(
            ((flow_hbm, flow_ref), (grid_hbm, grid_ref), (volume_hbm, volume_ref))
        )
    ]
    for load in loads:
        load.start()
    barrier = pltpu.get_barrier_semaphore()
    for s in range(1, n):
        pl.semaphore_signal(barrier, inc=1, device_id={"inst": peer(s)})
    pl.semaphore_signal(barrier, inc=1, device_id={"space": other})
    for load in loads:
        load.wait()
    for edge, row in ((0, rows - 1), (1, 0)):
        for v in range(variables):
            edge_out[edge, v : v + 1, :] = flow_ref[v, row : row + 1, :]
        for v in range(2):
            edge_out[edge, variables + v : variables + v + 1, :] = grid_ref[v, row : row + 1, :]
        edge_out[edge, variables + 2 : variables + 3, :] = jnp.zeros((1, columns), jnp.float32)
    pl.semaphore_wait(barrier, n)

    edges = pltpu.make_async_remote_copy(
        src_ref=edge_out,
        dst_ref=edge_in,
        send_sem=edge_send,
        recv_sem=edge_recv,
        device_id={"space": other},
    )
    edges.start()
    for c in range(variables):
        for s in order:
            pltpu.make_async_remote_copy(
                src_ref=flow_ref.at[c, :, columns_of(s)],
                dst_ref=slabs.at[c, s - 1],
                send_sem=slab_send,
                recv_sem=slab_recv.at[c],
                device_id={"inst": peer(s)},
            ).start()

    state = [flow_ref[v] for v in range(variables)]
    grid_0, grid_1, volume = grid_ref[0], grid_ref[1], volume_ref[...]
    speed_0, speed_1, pressure, sound = cell_terms(state)
    wave = jnp.abs(speed_0 - grid_0) + jnp.abs(speed_1 - grid_1) + 2.0 * sound
    push = (section_weight * courant_number) / (wave + math.pi * volume)
    step_ref[...] = push * volume

    lane = lax.broadcasted_iota(jnp.int32, (rows, columns), 1)
    own = (state, speed_1, pressure, sound, grid_1)
    left = on_side(lambda x: jnp.where(lane == 0, x, pltpu.roll(x, 1, 1)), own)
    flux = rusanov(left, own, 1)
    end = on_side(lambda x: x[:, columns - LANES :], own)
    last = rusanov(end, end, 1)
    lane_end = lane[:, columns - LANES :]
    for v in range(variables):
        upper = pltpu.roll(flux[v], columns - 1, 1)
        upper_end = jnp.where(lane_end == columns - 1, last[v], upper[:, columns - LANES :])
        upper = jnp.concatenate([upper[:, : columns - LANES], upper_end], axis=1)
        next_ref[v] = state[v] - push * (upper - flux[v])

    edges.wait_recv()

    def edge_side(edge):
        edge_state = [edge_in[edge, v : v + 1, :] for v in range(variables)]
        speed, _, edge_pressure, edge_sound = cell_terms(edge_state)
        grid = edge_in[edge, variables : variables + 1, :]
        return (edge_state, speed, edge_pressure, edge_sound, grid)

    above, below = edge_side(0), edge_side(1)
    row = lax.broadcasted_iota(jnp.int32, (rows, columns), 0)
    own = (state, speed_0, pressure, sound, grid_0)
    rolled = on_side(lambda x: pltpu.roll(x, 1, 0), own)
    first = lambda x, y: jnp.where(row == 0, y, x)
    left = (
        [first(x, y) for x, y in zip(rolled[0], above[0])],
    ) + tuple(first(x, y) for x, y in zip(rolled[1:], above[1:]))
    flux = rusanov(left, own, 0)
    last = rusanov(on_side(lambda x: x[rows - 1 : rows], own), below, 0)
    for v in range(variables):
        upper = jnp.where(row == rows - 1, last[v], pltpu.roll(flux[v], rows - 1, 0))
        next_ref[v] = next_ref[v] - push * (upper - flux[v])

    for c in range(variables):
        got = slabs.at[c]
        pltpu.make_async_remote_copy(
            src_ref=got,
            dst_ref=got,
            send_sem=slab_send,
            recv_sem=slab_recv.at[c],
            device_id={"inst": peer(1)},
        ).wait_recv()
        held = [flow_ref[c, :, columns_of(0)]] + [slabs[c, s - 1] for s in range(1, n)]
        mean_ref[c] = functools.reduce(jnp.add, held) * (1.0 / n)

        def rate(t):
            terms = [held[s] * spectral_weight((s - t) % n, n) for s in range(n) if s != t]
            return functools.reduce(jnp.add, terms)

        for t in order:
            rates[c, t - 1] = rate(t)
            pltpu.make_async_remote_copy(
                src_ref=rates.at[c, t - 1],
                dst_ref=returned.at[c, t - 1],
                send_sem=rate_send,
                recv_sem=rate_recv.at[c],
                device_id={"inst": peer(-t)},
            ).start()
        at = columns_of(0)
        next_ref[c, :, at] = next_ref[c, :, at] - step_ref[:, at] * rate(0)

    for c in range(variables):
        got = returned.at[c]
        pltpu.make_async_remote_copy(
            src_ref=got,
            dst_ref=got,
            send_sem=rate_send,
            recv_sem=rate_recv.at[c],
            device_id={"inst": peer(1)},
        ).wait_recv()
        for t in range(1, n):
            at = columns_of(t)
            next_ref[c, :, at] = next_ref[c, :, at] - step_ref[:, at] * returned[c, t - 1]

    edges.wait_send()
    for sent, sem in ((slabs, slab_send), (rates, rate_send)):
        pltpu.make_async_remote_copy(
            src_ref=sent,
            dst_ref=sent,
            send_sem=sem,
            recv_sem=edge_recv,
            device_id={"inst": peer(1)},
        ).wait_send()


def kernel_body(flow, grid_velocity, cell_volume):
    n = lax.axis_size("inst")
    variables, rows, columns = flow.shape[1:]
    width = columns // n
    f32 = jnp.float32
    exchanged = pltpu.VMEM((variables, n - 1, rows, width), f32)
    edge = pltpu.VMEM((2, variables + 3, columns), f32)
    dma = pltpu.SemaphoreType.DMA
    flow_next, mean_flow = pl.pallas_call(
        functools.partial(section_kernel, n),
        out_shape=(
            jax.ShapeDtypeStruct((variables, rows, columns), f32),
            jax.ShapeDtypeStruct((variables, rows, width), f32),
        ),
        in_specs=[pl.BlockSpec(memory_space=pltpu.HBM)] * 3,
        out_specs=[pl.BlockSpec(memory_space=pltpu.VMEM)] * 2,
        scratch_shapes=[
            pltpu.VMEM((variables, rows, columns), f32),
            pltpu.VMEM((2, rows, columns), f32),
            pltpu.VMEM((rows, columns), f32),
            exchanged,
            exchanged,
            exchanged,
            pltpu.VMEM((rows, columns), f32),
            edge,
            edge,
            dma,
            dma,
            dma,
            dma((variables,)),
            dma,
            dma((variables,)),
            dma((3,)),
        ],
        compiler_params=pltpu.CompilerParams(
            collective_id=0, has_side_effects=True, vmem_limit_bytes=32 * 1024 * 1024
        ),
        name="section",
    )(*[pltpu.with_memory_space_constraint(x, pltpu.HBM) for x in (flow[0], grid_velocity[0], cell_volume)])
    return flow_next[None], mean_flow


def solution(mesh):
    in_specs = (
        P(("groups", "inst"), None, "space", None),
        P(("groups", "inst"), None, "space", None),
        P("space", None),
    )
    out_specs = (P(("groups", "inst"), None, "space", None), P("groups", "space", "inst"))

    def local(flow, grid_velocity, cell_volume):
        whole_lanes = flow.shape[3] % (LANES * mesh.shape["inst"]) == 0
        whole_rows = flow.shape[2] % 8 == 0 and flow.shape[2] >= 8
        fits = mesh.shape["space"] == 2 and mesh.shape["inst"] > 1 and flow.shape[0] == 1
        chosen = kernel_body if whole_lanes and whole_rows and fits else body
        return chosen(flow, grid_velocity, cell_volume)

    return jax.shard_map(local, mesh=mesh, in_specs=in_specs, out_specs=out_specs, check_vma=False)
```

```python
import functools
import math

import jax
import jax.numpy as jnp
import numpy as np
from jax import lax
from jax.experimental import pallas as pl
from jax.experimental.pallas import tpu as pltpu
from jax.sharding import PartitionSpec as P

gamma_ratio = 1.4
courant_number = 1.5
section_weight = 0.5


def extended_2(x, sides, width):
    for axis, dim in sides:
        devices, length = (lax.axis_size(axis), x.shape[dim])
        up = [(i, (i + 1) % devices) for i in range(devices)]
        down = [(j, i) for i, j in up]
        last = lax.slice_in_dim(x, length - width, length, axis=dim)
        leading = lax.slice_in_dim(x, 0, width, axis=dim)
        before = lax.ppermute(last, axis, up)
        after = lax.ppermute(leading, axis, down)
        x = jnp.concatenate([before, x, after], axis=dim)
    return x


def coefficient(offsets, inst_count):
    parity = (offsets % 2).astype(jnp.float32)
    angle = math.pi / inst_count * offsets.astype(jnp.float32)
    safe_sine = jnp.where(offsets == 0, 1.0, jnp.sin(angle))
    value = (1.0 - 2.0 * parity) * (math.pi / inst_count) * jnp.cos(angle) / safe_sine
    return jnp.where(offsets == 0, 0.0, value)


def cell_state(state):
    density = state[:, 0]
    velocity = state[:, 1:4] / density[:, None]
    kinetic = 0.5 * jnp.sum(state[:, 1:4] * velocity, axis=1)
    pressure = (gamma_ratio - 1.0) * (state[:, 4] - kinetic)
    sound = jnp.sqrt(gamma_ratio * pressure / density)
    return (velocity, pressure, sound)


def side_flux(state, face_speed, normal):
    velocity, pressure, sound = cell_state(state)
    normal_speed = velocity[:, normal]
    relative = normal_speed - face_speed
    unit_push = jnp.asarray(np.eye(5, dtype=np.float32)[1 + normal]).reshape(1, 5, 1, 1)
    unit_work = jnp.asarray(np.eye(5, dtype=np.float32)[4]).reshape(1, 5, 1, 1)
    flux = (
        state * relative[:, None]
        + pressure[:, None] * unit_push
        + (pressure * normal_speed)[:, None] * unit_work
    )
    return (flux, jnp.abs(relative) + sound)


def face_flux(left_state, right_state, left_grid, right_grid, normal):
    face_speed = 0.5 * (left_grid[:, normal] + right_grid[:, normal])
    flux_left, reach_left = side_flux(left_state, face_speed, normal)
    flux_right, reach_right = side_flux(right_state, face_speed, normal)
    reach = jnp.maximum(reach_left, reach_right)
    return 0.5 * (flux_left + flux_right) - 0.5 * reach[:, None] * (right_state - left_state)


def section_update(flow, grid_velocity, cell_volume, ext_state, ext_grid, derivative):
    flux_x = face_flux(
        ext_state[:, :, :-1], ext_state[:, :, 1:], ext_grid[:, :, :-1], ext_grid[:, :, 1:], 0
    )
    state_y = jnp.concatenate([flow[..., :1], flow, flow[..., -1:]], axis=3)
    grid_y = jnp.concatenate(
        [grid_velocity[..., :1], grid_velocity, grid_velocity[..., -1:]], axis=3
    )
    flux_y = face_flux(state_y[..., :-1], state_y[..., 1:], grid_y[..., :-1], grid_y[..., 1:], 1)
    divergence = (
        flux_x[:, :, 1:] - flux_x[:, :, :-1] + flux_y[..., 1:] - flux_y[..., :-1]
    ) / cell_volume
    residual = derivative + divergence
    velocity, pressure, sound = cell_state(flow)
    reach_sum = (
        jnp.abs(velocity[:, 0] - grid_velocity[:, 0])
        + jnp.abs(velocity[:, 1] - grid_velocity[:, 1])
        + 2.0 * sound
    )
    pseudo_step = courant_number * cell_volume / (reach_sum + math.pi * cell_volume)
    return flow - section_weight * pseudo_step[:, None] * residual


def body(flow, grid_velocity, cell_volume):
    inst_count = lax.axis_size("inst")
    own_index = lax.axis_index("inst")
    packed = jnp.concatenate([flow, grid_velocity], axis=1)
    extended = extended_2(packed, (("space", 2),), 1)
    ext_state = extended[:, :5]
    ext_grid = extended[:, 5:]
    slices = lax.all_gather(flow, "inst", axis=0, tiled=True)
    positions = jnp.arange(slices.shape[0], dtype=jnp.int32)
    weights = coefficient((own_index - positions) % inst_count, inst_count)
    added = jnp.einsum("j,jvxy->vxy", weights, slices, precision=lax.Precision.HIGHEST)
    derivative = added[None]
    summed = jnp.sum(slices, axis=0, keepdims=True)
    slab_width = flow.shape[3] // inst_count
    mean_flow = (
        lax.dynamic_slice_in_dim(summed[0], own_index * slab_width, slab_width, 2) / inst_count
    )
    flow_next = section_update(flow, grid_velocity, cell_volume, ext_state, ext_grid, derivative)
    return (flow_next, mean_flow)


LANES = 128


def spectral_weight(offset, count):
    if offset == 0:
        return 0.0
    angle = math.pi * offset / count
    return (-1.0) ** offset * (math.pi / count) * math.cos(angle) / math.sin(angle)


def cell_terms(state):
    inverse = 1.0 / state[0]
    speeds = [state[k] * inverse for k in (1, 2, 3)]
    kinetic = 0.5 * (state[1] * speeds[0] + state[2] * speeds[1] + state[3] * speeds[2])
    pressure = (gamma_ratio - 1.0) * (state[4] - kinetic)
    sound = jnp.sqrt(gamma_ratio * pressure * inverse)
    return speeds[0], speeds[1], pressure, sound


def rusanov(left, right, normal):
    state_l, speed_l, pressure_l, sound_l, grid_l = left
    state_r, speed_r, pressure_r, sound_r, grid_r = right
    face_speed = 0.5 * (grid_l + grid_r)
    relative_l = speed_l - face_speed
    relative_r = speed_r - face_speed
    reach = jnp.maximum(jnp.abs(relative_l) + sound_l, jnp.abs(relative_r) + sound_r)
    weight_l = 0.5 * (relative_l + reach)
    weight_r = 0.5 * (relative_r - reach)
    flux = [a * weight_l + b * weight_r for a, b in zip(state_l, state_r)]
    flux[1 + normal] += 0.5 * (pressure_l + pressure_r)
    flux[4] += 0.5 * (pressure_l * speed_l + pressure_r * speed_r)
    return flux


def on_side(change, side):
    return ([change(x) for x in side[0]],) + tuple(change(x) for x in side[1:])


def section_kernel(
    n,
    flow_hbm,
    grid_hbm,
    volume_hbm,
    next_ref,
    mean_ref,
    flow_ref,
    grid_ref,
    volume_ref,
    slabs,
    rates,
    returned,
    step_ref,
    edge_out,
    edge_in,
    edge_send,
    edge_recv,
    slab_send,
    slab_recv,
    rate_send,
    rate_recv,
    load_sem,
):
    variables, rows, columns = flow_ref.shape
    width = columns // n
    me = lax.axis_index("inst")
    other = 1 - lax.axis_index("space")
    order = sorted(range(1, n), key=lambda s: abs(2 * s - n))

    def peer(offset):
        return lax.rem(me + (offset + n), n)

    def columns_of(offset):
        return pl.ds(pl.multiple_of(peer(offset) * width, width), width)

    loads = [
        pltpu.make_async_copy(source, target, load_sem.at[k])
        for k, (source, target) in enumerate(
            ((flow_hbm, flow_ref), (grid_hbm, grid_ref), (volume_hbm, volume_ref))
        )
    ]
    for load in loads:
        load.start()
    barrier = pltpu.get_barrier_semaphore()
    for s in range(1, n):
        pl.semaphore_signal(barrier, inc=1, device_id={"inst": peer(s)})
    pl.semaphore_signal(barrier, inc=1, device_id={"space": other})
    for load in loads:
        load.wait()
    for edge, row in ((0, rows - 1), (1, 0)):
        for v in range(variables):
            edge_out[edge, v : v + 1, :] = flow_ref[v, row : row + 1, :]
        for v in range(2):
            edge_out[edge, variables + v : variables + v + 1, :] = grid_ref[v, row : row + 1, :]
        edge_out[edge, variables + 2 : variables + 3, :] = jnp.zeros((1, columns), jnp.float32)
    pl.semaphore_wait(barrier, n)

    edges = pltpu.make_async_remote_copy(
        src_ref=edge_out,
        dst_ref=edge_in,
        send_sem=edge_send,
        recv_sem=edge_recv,
        device_id={"space": other},
    )
    edges.start()
    for c in range(variables):
        for s in order:
            pltpu.make_async_remote_copy(
                src_ref=flow_ref.at[c, :, columns_of(s)],
                dst_ref=slabs.at[c, s - 1],
                send_sem=slab_send,
                recv_sem=slab_recv.at[c],
                device_id={"inst": peer(s)},
            ).start()

    state = [flow_ref[v] for v in range(variables)]
    grid_0, grid_1, volume = grid_ref[0], grid_ref[1], volume_ref[...]
    speed_0, speed_1, pressure, sound = cell_terms(state)
    wave = jnp.abs(speed_0 - grid_0) + jnp.abs(speed_1 - grid_1) + 2.0 * sound
    push = (section_weight * courant_number) / (wave + math.pi * volume)
    step_ref[...] = push * volume

    lane = lax.broadcasted_iota(jnp.int32, (rows, columns), 1)
    own = (state, speed_1, pressure, sound, grid_1)
    left = on_side(lambda x: jnp.where(lane == 0, x, pltpu.roll(x, 1, 1)), own)
    flux = rusanov(left, own, 1)
    end = on_side(lambda x: x[:, columns - LANES :], own)
    last = rusanov(end, end, 1)
    lane_end = lane[:, columns - LANES :]
    for v in range(variables):
        upper = pltpu.roll(flux[v], columns - 1, 1)
        upper_end = jnp.where(lane_end == columns - 1, last[v], upper[:, columns - LANES :])
        upper = jnp.concatenate([upper[:, : columns - LANES], upper_end], axis=1)
        next_ref[v] = state[v] - push * (upper - flux[v])

    edges.wait_recv()

    def edge_side(edge):
        edge_state = [edge_in[edge, v : v + 1, :] for v in range(variables)]
        speed, _, edge_pressure, edge_sound = cell_terms(edge_state)
        grid = edge_in[edge, variables : variables + 1, :]
        return (edge_state, speed, edge_pressure, edge_sound, grid)

    above, below = edge_side(0), edge_side(1)
    row = lax.broadcasted_iota(jnp.int32, (rows, columns), 0)
    own = (state, speed_0, pressure, sound, grid_0)
    rolled = on_side(lambda x: pltpu.roll(x, 1, 0), own)
    first = lambda x, y: jnp.where(row == 0, y, x)
    left = (
        [first(x, y) for x, y in zip(rolled[0], above[0])],
    ) + tuple(first(x, y) for x, y in zip(rolled[1:], above[1:]))
    flux = rusanov(left, own, 0)
    last = rusanov(on_side(lambda x: x[rows - 1 : rows], own), below, 0)
    for v in range(variables):
        upper = jnp.where(row == rows - 1, last[v], pltpu.roll(flux[v], rows - 1, 0))
        next_ref[v] = next_ref[v] - push * (upper - flux[v])

    for c in range(variables):
        got = slabs.at[c]
        pltpu.make_async_remote_copy(
            src_ref=got,
            dst_ref=got,
            send_sem=slab_send,
            recv_sem=slab_recv.at[c],
            device_id={"inst": peer(1)},
        ).wait_recv()
        held = [flow_ref[c, :, columns_of(0)]] + [slabs[c, s - 1] for s in range(1, n)]
        mean_ref[c] = functools.reduce(jnp.add, held) * (1.0 / n)

        def rate(t):
            terms = [held[s] * spectral_weight((s - t) % n, n) for s in range(n) if s != t]
            return functools.reduce(jnp.add, terms)

        for t in order:
            rates[c, t - 1] = rate(t)
            pltpu.make_async_remote_copy(
                src_ref=rates.at[c, t - 1],
                dst_ref=returned.at[c, t - 1],
                send_sem=rate_send,
                recv_sem=rate_recv.at[c],
                device_id={"inst": peer(-t)},
            ).start()
        at = columns_of(0)
        next_ref[c, :, at] = next_ref[c, :, at] - step_ref[:, at] * rate(0)

    for c in range(variables):
        got = returned.at[c]
        pltpu.make_async_remote_copy(
            src_ref=got,
            dst_ref=got,
            send_sem=rate_send,
            recv_sem=rate_recv.at[c],
            device_id={"inst": peer(1)},
        ).wait_recv()
        for t in range(1, n):
            at = columns_of(t)
            next_ref[c, :, at] = next_ref[c, :, at] - step_ref[:, at] * returned[c, t - 1]

    edges.wait_send()
    for sent, sem in ((slabs, slab_send), (rates, rate_send)):
        pltpu.make_async_remote_copy(
            src_ref=sent,
            dst_ref=sent,
            send_sem=sem,
            recv_sem=edge_recv,
            device_id={"inst": peer(1)},
        ).wait_send()


def write_kernel(next_ref, mean_ref, next_hbm, mean_hbm, sems):
    writes = [
        pltpu.make_async_copy(next_ref, next_hbm, sems.at[0]),
        pltpu.make_async_copy(mean_ref, mean_hbm, sems.at[1]),
    ]
    for write in writes:
        write.start()
    for write in writes:
        write.wait()


def kernel_body(flow, grid_velocity, cell_volume):
    n = lax.axis_size("inst")
    variables, rows, columns = flow.shape[1:]
    width = columns // n
    f32 = jnp.float32
    exchanged = pltpu.VMEM((variables, n - 1, rows, width), f32)
    edge = pltpu.VMEM((2, variables + 3, columns), f32)
    dma = pltpu.SemaphoreType.DMA
    flow_next, mean_flow = pl.pallas_call(
        functools.partial(section_kernel, n),
        out_shape=(
            pltpu.VMEM((variables, rows, columns), f32),
            pltpu.VMEM((variables, rows, width), f32),
        ),
        in_specs=[pl.BlockSpec(memory_space=pltpu.HBM)] * 3,
        out_specs=[pl.BlockSpec(memory_space=pltpu.VMEM)] * 2,
        scratch_shapes=[
            pltpu.VMEM((variables, rows, columns), f32),
            pltpu.VMEM((2, rows, columns), f32),
            pltpu.VMEM((rows, columns), f32),
            exchanged,
            exchanged,
            exchanged,
            pltpu.VMEM((rows, columns), f32),
            edge,
            edge,
            dma,
            dma,
            dma,
            dma((variables,)),
            dma,
            dma((variables,)),
            dma((3,)),
        ],
        compiler_params=pltpu.CompilerParams(
            collective_id=0, has_side_effects=True, vmem_limit_bytes=32 * 1024 * 1024
        ),
        name="section",
    )(*[pltpu.with_memory_space_constraint(x, pltpu.HBM) for x in (flow[0], grid_velocity[0], cell_volume)])
    flow_next, mean_flow = pl.pallas_call(
        write_kernel,
        out_shape=(
            jax.ShapeDtypeStruct(flow_next.shape, f32),
            jax.ShapeDtypeStruct(mean_flow.shape, f32),
        ),
        in_specs=[pl.BlockSpec(memory_space=pltpu.VMEM)] * 2,
        out_specs=[pl.BlockSpec(memory_space=pltpu.HBM)] * 2,
        scratch_shapes=[dma((2,))],
        name="write",
    )(*[pltpu.with_memory_space_constraint(x, pltpu.VMEM) for x in (flow_next, mean_flow)])
    return flow_next[None], mean_flow


def solution(mesh):
    in_specs = (
        P(("groups", "inst"), None, "space", None),
        P(("groups", "inst"), None, "space", None),
        P("space", None),
    )
    out_specs = (P(("groups", "inst"), None, "space", None), P("groups", "space", "inst"))

    def local(flow, grid_velocity, cell_volume):
        whole_lanes = flow.shape[3] % (LANES * mesh.shape["inst"]) == 0
        whole_rows = flow.shape[2] % 8 == 0 and flow.shape[2] >= 8
        fits = mesh.shape["space"] == 2 and mesh.shape["inst"] > 1 and flow.shape[0] == 1
        chosen = kernel_body if whole_lanes and whole_rows and fits else body
        return chosen(flow, grid_velocity, cell_volume)

    return jax.shard_map(local, mesh=mesh, in_specs=in_specs, out_specs=out_specs, check_vma=False)
```

```python
import functools
import math

import jax
import jax.numpy as jnp
import numpy as np
from jax import lax
from jax.experimental import pallas as pl
from jax.experimental.pallas import tpu as pltpu
from jax.sharding import PartitionSpec as P

gamma_ratio = 1.4
courant_number = 1.5
section_weight = 0.5


def extended_2(x, sides, width):
    for axis, dim in sides:
        devices, length = (lax.axis_size(axis), x.shape[dim])
        up = [(i, (i + 1) % devices) for i in range(devices)]
        down = [(j, i) for i, j in up]
        last = lax.slice_in_dim(x, length - width, length, axis=dim)
        leading = lax.slice_in_dim(x, 0, width, axis=dim)
        before = lax.ppermute(last, axis, up)
        after = lax.ppermute(leading, axis, down)
        x = jnp.concatenate([before, x, after], axis=dim)
    return x


def coefficient(offsets, inst_count):
    parity = (offsets % 2).astype(jnp.float32)
    angle = math.pi / inst_count * offsets.astype(jnp.float32)
    safe_sine = jnp.where(offsets == 0, 1.0, jnp.sin(angle))
    value = (1.0 - 2.0 * parity) * (math.pi / inst_count) * jnp.cos(angle) / safe_sine
    return jnp.where(offsets == 0, 0.0, value)


def cell_state(state):
    density = state[:, 0]
    velocity = state[:, 1:4] / density[:, None]
    kinetic = 0.5 * jnp.sum(state[:, 1:4] * velocity, axis=1)
    pressure = (gamma_ratio - 1.0) * (state[:, 4] - kinetic)
    sound = jnp.sqrt(gamma_ratio * pressure / density)
    return (velocity, pressure, sound)


def side_flux(state, face_speed, normal):
    velocity, pressure, sound = cell_state(state)
    normal_speed = velocity[:, normal]
    relative = normal_speed - face_speed
    unit_push = jnp.asarray(np.eye(5, dtype=np.float32)[1 + normal]).reshape(1, 5, 1, 1)
    unit_work = jnp.asarray(np.eye(5, dtype=np.float32)[4]).reshape(1, 5, 1, 1)
    flux = (
        state * relative[:, None]
        + pressure[:, None] * unit_push
        + (pressure * normal_speed)[:, None] * unit_work
    )
    return (flux, jnp.abs(relative) + sound)


def face_flux(left_state, right_state, left_grid, right_grid, normal):
    face_speed = 0.5 * (left_grid[:, normal] + right_grid[:, normal])
    flux_left, reach_left = side_flux(left_state, face_speed, normal)
    flux_right, reach_right = side_flux(right_state, face_speed, normal)
    reach = jnp.maximum(reach_left, reach_right)
    return 0.5 * (flux_left + flux_right) - 0.5 * reach[:, None] * (right_state - left_state)


def section_update(flow, grid_velocity, cell_volume, ext_state, ext_grid, derivative):
    flux_x = face_flux(
        ext_state[:, :, :-1], ext_state[:, :, 1:], ext_grid[:, :, :-1], ext_grid[:, :, 1:], 0
    )
    state_y = jnp.concatenate([flow[..., :1], flow, flow[..., -1:]], axis=3)
    grid_y = jnp.concatenate(
        [grid_velocity[..., :1], grid_velocity, grid_velocity[..., -1:]], axis=3
    )
    flux_y = face_flux(state_y[..., :-1], state_y[..., 1:], grid_y[..., :-1], grid_y[..., 1:], 1)
    divergence = (
        flux_x[:, :, 1:] - flux_x[:, :, :-1] + flux_y[..., 1:] - flux_y[..., :-1]
    ) / cell_volume
    residual = derivative + divergence
    velocity, pressure, sound = cell_state(flow)
    reach_sum = (
        jnp.abs(velocity[:, 0] - grid_velocity[:, 0])
        + jnp.abs(velocity[:, 1] - grid_velocity[:, 1])
        + 2.0 * sound
    )
    pseudo_step = courant_number * cell_volume / (reach_sum + math.pi * cell_volume)
    return flow - section_weight * pseudo_step[:, None] * residual


def body(flow, grid_velocity, cell_volume):
    inst_count = lax.axis_size("inst")
    own_index = lax.axis_index("inst")
    packed = jnp.concatenate([flow, grid_velocity], axis=1)
    extended = extended_2(packed, (("space", 2),), 1)
    ext_state = extended[:, :5]
    ext_grid = extended[:, 5:]
    slices = lax.all_gather(flow, "inst", axis=0, tiled=True)
    positions = jnp.arange(slices.shape[0], dtype=jnp.int32)
    weights = coefficient((own_index - positions) % inst_count, inst_count)
    added = jnp.einsum("j,jvxy->vxy", weights, slices, precision=lax.Precision.HIGHEST)
    derivative = added[None]
    summed = jnp.sum(slices, axis=0, keepdims=True)
    slab_width = flow.shape[3] // inst_count
    mean_flow = (
        lax.dynamic_slice_in_dim(summed[0], own_index * slab_width, slab_width, 2) / inst_count
    )
    flow_next = section_update(flow, grid_velocity, cell_volume, ext_state, ext_grid, derivative)
    return (flow_next, mean_flow)


LANES = 128
PIECES = 2


def spectral_weight(offset, count):
    if offset == 0:
        return 0.0
    angle = math.pi * offset / count
    return (-1.0) ** offset * (math.pi / count) * math.cos(angle) / math.sin(angle)


def cell_terms(state):
    inverse = 1.0 / state[0]
    speeds = [state[k] * inverse for k in (1, 2, 3)]
    kinetic = 0.5 * (state[1] * speeds[0] + state[2] * speeds[1] + state[3] * speeds[2])
    pressure = (gamma_ratio - 1.0) * (state[4] - kinetic)
    sound = jnp.sqrt(gamma_ratio * pressure * inverse)
    return speeds[0], speeds[1], pressure, sound


def rusanov(left, right, normal):
    state_l, speed_l, pressure_l, sound_l, grid_l = left
    state_r, speed_r, pressure_r, sound_r, grid_r = right
    face_speed = 0.5 * (grid_l + grid_r)
    relative_l = speed_l - face_speed
    relative_r = speed_r - face_speed
    reach = jnp.maximum(jnp.abs(relative_l) + sound_l, jnp.abs(relative_r) + sound_r)
    weight_l = 0.5 * (relative_l + reach)
    weight_r = 0.5 * (relative_r - reach)
    flux = [a * weight_l + b * weight_r for a, b in zip(state_l, state_r)]
    flux[1 + normal] += 0.5 * (pressure_l + pressure_r)
    flux[4] += 0.5 * (pressure_l * speed_l + pressure_r * speed_r)
    return flux


def on_side(change, side):
    return ([change(x) for x in side[0]],) + tuple(change(x) for x in side[1:])


def section_kernel(
    n,
    flow_hbm,
    grid_hbm,
    volume_hbm,
    next_ref,
    mean_ref,
    flow_ref,
    grid_ref,
    volume_ref,
    slabs,
    rates,
    returned,
    step_ref,
    edge_out,
    edge_in,
    edge_send,
    edge_recv,
    slab_send,
    slab_recv,
    rate_send,
    rate_recv,
    load_sem,
):
    variables, rows, columns = flow_ref.shape
    width = columns // n
    me = lax.axis_index("inst")
    other = 1 - lax.axis_index("space")
    order = sorted(range(1, n), key=lambda s: abs(2 * s - n))

    def peer(offset):
        return lax.rem(me + (offset + n), n)

    def columns_of(offset):
        return pl.ds(pl.multiple_of(peer(offset) * width, width), width)

    loads = [
        pltpu.make_async_copy(source, target, load_sem.at[k])
        for k, (source, target) in enumerate(
            ((flow_hbm, flow_ref), (grid_hbm, grid_ref), (volume_hbm, volume_ref))
        )
    ]
    for load in loads:
        load.start()
    barrier = pltpu.get_barrier_semaphore()
    for s in range(1, n):
        pl.semaphore_signal(barrier, inc=1, device_id={"inst": peer(s)})
    pl.semaphore_signal(barrier, inc=1, device_id={"space": other})
    for load in loads:
        load.wait()
    for edge, row in ((0, rows - 1), (1, 0)):
        for v in range(variables):
            edge_out[edge, v : v + 1, :] = flow_ref[v, row : row + 1, :]
        for v in range(2):
            edge_out[edge, variables + v : variables + v + 1, :] = grid_ref[v, row : row + 1, :]
        edge_out[edge, variables + 2 : variables + 3, :] = jnp.zeros((1, columns), jnp.float32)
    pl.semaphore_wait(barrier, n)

    edges = pltpu.make_async_remote_copy(
        src_ref=edge_out,
        dst_ref=edge_in,
        send_sem=edge_send,
        recv_sem=edge_recv,
        device_id={"space": other},
    )
    edges.start()
    cuts = [-(-variables * k // PIECES) for k in range(PIECES + 1)]
    pieces = list(enumerate(slice(a, b) for a, b in zip(cuts, cuts[1:])))
    for k, c in pieces:
        for s in order:
            pltpu.make_async_remote_copy(
                src_ref=flow_ref.at[c, :, columns_of(s)],
                dst_ref=slabs.at[s - 1, c],
                send_sem=slab_send,
                recv_sem=slab_recv.at[k],
                device_id={"inst": peer(s)},
            ).start()

    state = [flow_ref[v] for v in range(variables)]
    grid_0, grid_1, volume = grid_ref[0], grid_ref[1], volume_ref[...]
    speed_0, speed_1, pressure, sound = cell_terms(state)
    wave = jnp.abs(speed_0 - grid_0) + jnp.abs(speed_1 - grid_1) + 2.0 * sound
    push = (section_weight * courant_number) / (wave + math.pi * volume)
    step_ref[...] = push * volume

    lane = lax.broadcasted_iota(jnp.int32, (rows, columns), 1)
    own = (state, speed_1, pressure, sound, grid_1)
    left = on_side(lambda x: jnp.where(lane == 0, x, pltpu.roll(x, 1, 1)), own)
    flux = rusanov(left, own, 1)
    end = on_side(lambda x: x[:, columns - LANES :], own)
    last = rusanov(end, end, 1)
    lane_end = lane[:, columns - LANES :]
    for v in range(variables):
        upper = pltpu.roll(flux[v], columns - 1, 1)
        upper_end = jnp.where(lane_end == columns - 1, last[v], upper[:, columns - LANES :])
        upper = jnp.concatenate([upper[:, : columns - LANES], upper_end], axis=1)
        next_ref[v] = state[v] - push * (upper - flux[v])

    edges.wait_recv()

    def edge_side(edge):
        edge_state = [edge_in[edge, v : v + 1, :] for v in range(variables)]
        speed, _, edge_pressure, edge_sound = cell_terms(edge_state)
        grid = edge_in[edge, variables : variables + 1, :]
        return (edge_state, speed, edge_pressure, edge_sound, grid)

    above, below = edge_side(0), edge_side(1)
    row = lax.broadcasted_iota(jnp.int32, (rows, columns), 0)
    own = (state, speed_0, pressure, sound, grid_0)
    rolled = on_side(lambda x: pltpu.roll(x, 1, 0), own)
    first = lambda x, y: jnp.where(row == 0, y, x)
    left = (
        [first(x, y) for x, y in zip(rolled[0], above[0])],
    ) + tuple(first(x, y) for x, y in zip(rolled[1:], above[1:]))
    flux = rusanov(left, own, 0)
    last = rusanov(on_side(lambda x: x[rows - 1 : rows], own), below, 0)
    for v in range(variables):
        upper = jnp.where(row == rows - 1, last[v], pltpu.roll(flux[v], rows - 1, 0))
        next_ref[v] = next_ref[v] - push * (upper - flux[v])

    for k, c in pieces:
        got = slabs.at[:, c]
        pltpu.make_async_remote_copy(
            src_ref=got,
            dst_ref=got,
            send_sem=slab_send,
            recv_sem=slab_recv.at[k],
            device_id={"inst": peer(1)},
        ).wait_recv()
        held = [flow_ref[c, :, columns_of(0)]] + [slabs[s - 1, c] for s in range(1, n)]
        mean_ref[c] = functools.reduce(jnp.add, held) * (1.0 / n)

        def rate(t):
            terms = [held[s] * spectral_weight((s - t) % n, n) for s in range(n) if s != t]
            return functools.reduce(jnp.add, terms)

        for t in order:
            rates[t - 1, c] = rate(t)
            pltpu.make_async_remote_copy(
                src_ref=rates.at[t - 1, c],
                dst_ref=returned.at[t - 1, c],
                send_sem=rate_send,
                recv_sem=rate_recv.at[k],
                device_id={"inst": peer(-t)},
            ).start()
        at = columns_of(0)
        next_ref[c, :, at] = next_ref[c, :, at] - step_ref[:, at] * rate(0)

    for k, c in pieces:
        got = returned.at[:, c]
        pltpu.make_async_remote_copy(
            src_ref=got,
            dst_ref=got,
            send_sem=rate_send,
            recv_sem=rate_recv.at[k],
            device_id={"inst": peer(1)},
        ).wait_recv()
        for t in range(1, n):
            at = columns_of(t)
            next_ref[c, :, at] = next_ref[c, :, at] - step_ref[:, at] * returned[t - 1, c]

    edges.wait_send()
    for sent, sem in ((slabs, slab_send), (rates, rate_send)):
        pltpu.make_async_remote_copy(
            src_ref=sent,
            dst_ref=sent,
            send_sem=sem,
            recv_sem=edge_recv,
            device_id={"inst": peer(1)},
        ).wait_send()


def write_kernel(next_ref, mean_ref, next_hbm, mean_hbm, sems):
    writes = [
        pltpu.make_async_copy(next_ref, next_hbm, sems.at[0]),
        pltpu.make_async_copy(mean_ref, mean_hbm, sems.at[1]),
    ]
    for write in writes:
        write.start()
    for write in writes:
        write.wait()


def kernel_body(flow, grid_velocity, cell_volume):
    n = lax.axis_size("inst")
    variables, rows, columns = flow.shape[1:]
    width = columns // n
    f32 = jnp.float32
    exchanged = pltpu.VMEM((n - 1, variables, rows, width), f32)
    edge = pltpu.VMEM((2, variables + 3, columns), f32)
    dma = pltpu.SemaphoreType.DMA
    flow_next, mean_flow = pl.pallas_call(
        functools.partial(section_kernel, n),
        out_shape=(
            pltpu.VMEM((variables, rows, columns), f32),
            pltpu.VMEM((variables, rows, width), f32),
        ),
        in_specs=[pl.BlockSpec(memory_space=pltpu.HBM)] * 3,
        out_specs=[pl.BlockSpec(memory_space=pltpu.VMEM)] * 2,
        scratch_shapes=[
            pltpu.VMEM((variables, rows, columns), f32),
            pltpu.VMEM((2, rows, columns), f32),
            pltpu.VMEM((rows, columns), f32),
            exchanged,
            exchanged,
            exchanged,
            pltpu.VMEM((rows, columns), f32),
            edge,
            edge,
            dma,
            dma,
            dma,
            dma((PIECES,)),
            dma,
            dma((PIECES,)),
            dma((3,)),
        ],
        compiler_params=pltpu.CompilerParams(
            collective_id=0, has_side_effects=True, vmem_limit_bytes=32 * 1024 * 1024
        ),
        name="section",
    )(*[pltpu.with_memory_space_constraint(x, pltpu.HBM) for x in (flow[0], grid_velocity[0], cell_volume)])
    flow_next, mean_flow = pl.pallas_call(
        write_kernel,
        out_shape=(
            jax.ShapeDtypeStruct(flow_next.shape, f32),
            jax.ShapeDtypeStruct(mean_flow.shape, f32),
        ),
        in_specs=[pl.BlockSpec(memory_space=pltpu.VMEM)] * 2,
        out_specs=[pl.BlockSpec(memory_space=pltpu.HBM)] * 2,
        scratch_shapes=[dma((2,))],
        name="write",
    )(*[pltpu.with_memory_space_constraint(x, pltpu.VMEM) for x in (flow_next, mean_flow)])
    return flow_next[None], mean_flow


def solution(mesh):
    in_specs = (
        P(("groups", "inst"), None, "space", None),
        P(("groups", "inst"), None, "space", None),
        P("space", None),
    )
    out_specs = (P(("groups", "inst"), None, "space", None), P("groups", "space", "inst"))

    def local(flow, grid_velocity, cell_volume):
        whole_lanes = flow.shape[3] % (LANES * mesh.shape["inst"]) == 0
        whole_rows = flow.shape[2] % 8 == 0 and flow.shape[2] >= 8
        fits = mesh.shape["space"] == 2 and mesh.shape["inst"] > 1 and flow.shape[0] == 1
        chosen = kernel_body if whole_lanes and whole_rows and fits else body
        return chosen(flow, grid_velocity, cell_volume)

    return jax.shard_map(local, mesh=mesh, in_specs=in_specs, out_specs=out_specs, check_vma=False)
```

```python
import functools
import math

import jax
import jax.numpy as jnp
import numpy as np
from jax import lax
from jax.experimental import pallas as pl
from jax.experimental.pallas import tpu as pltpu
from jax.sharding import PartitionSpec as P

gamma_ratio = 1.4
courant_number = 1.5
section_weight = 0.5


def extended_2(x, sides, width):
    for axis, dim in sides:
        devices, length = (lax.axis_size(axis), x.shape[dim])
        up = [(i, (i + 1) % devices) for i in range(devices)]
        down = [(j, i) for i, j in up]
        last = lax.slice_in_dim(x, length - width, length, axis=dim)
        leading = lax.slice_in_dim(x, 0, width, axis=dim)
        before = lax.ppermute(last, axis, up)
        after = lax.ppermute(leading, axis, down)
        x = jnp.concatenate([before, x, after], axis=dim)
    return x


def coefficient(offsets, inst_count):
    parity = (offsets % 2).astype(jnp.float32)
    angle = math.pi / inst_count * offsets.astype(jnp.float32)
    safe_sine = jnp.where(offsets == 0, 1.0, jnp.sin(angle))
    value = (1.0 - 2.0 * parity) * (math.pi / inst_count) * jnp.cos(angle) / safe_sine
    return jnp.where(offsets == 0, 0.0, value)


def cell_state(state):
    density = state[:, 0]
    velocity = state[:, 1:4] / density[:, None]
    kinetic = 0.5 * jnp.sum(state[:, 1:4] * velocity, axis=1)
    pressure = (gamma_ratio - 1.0) * (state[:, 4] - kinetic)
    sound = jnp.sqrt(gamma_ratio * pressure / density)
    return (velocity, pressure, sound)


def side_flux(state, face_speed, normal):
    velocity, pressure, sound = cell_state(state)
    normal_speed = velocity[:, normal]
    relative = normal_speed - face_speed
    unit_push = jnp.asarray(np.eye(5, dtype=np.float32)[1 + normal]).reshape(1, 5, 1, 1)
    unit_work = jnp.asarray(np.eye(5, dtype=np.float32)[4]).reshape(1, 5, 1, 1)
    flux = (
        state * relative[:, None]
        + pressure[:, None] * unit_push
        + (pressure * normal_speed)[:, None] * unit_work
    )
    return (flux, jnp.abs(relative) + sound)


def face_flux(left_state, right_state, left_grid, right_grid, normal):
    face_speed = 0.5 * (left_grid[:, normal] + right_grid[:, normal])
    flux_left, reach_left = side_flux(left_state, face_speed, normal)
    flux_right, reach_right = side_flux(right_state, face_speed, normal)
    reach = jnp.maximum(reach_left, reach_right)
    return 0.5 * (flux_left + flux_right) - 0.5 * reach[:, None] * (right_state - left_state)


def section_update(flow, grid_velocity, cell_volume, ext_state, ext_grid, derivative):
    flux_x = face_flux(
        ext_state[:, :, :-1], ext_state[:, :, 1:], ext_grid[:, :, :-1], ext_grid[:, :, 1:], 0
    )
    state_y = jnp.concatenate([flow[..., :1], flow, flow[..., -1:]], axis=3)
    grid_y = jnp.concatenate(
        [grid_velocity[..., :1], grid_velocity, grid_velocity[..., -1:]], axis=3
    )
    flux_y = face_flux(state_y[..., :-1], state_y[..., 1:], grid_y[..., :-1], grid_y[..., 1:], 1)
    divergence = (
        flux_x[:, :, 1:] - flux_x[:, :, :-1] + flux_y[..., 1:] - flux_y[..., :-1]
    ) / cell_volume
    residual = derivative + divergence
    velocity, pressure, sound = cell_state(flow)
    reach_sum = (
        jnp.abs(velocity[:, 0] - grid_velocity[:, 0])
        + jnp.abs(velocity[:, 1] - grid_velocity[:, 1])
        + 2.0 * sound
    )
    pseudo_step = courant_number * cell_volume / (reach_sum + math.pi * cell_volume)
    return flow - section_weight * pseudo_step[:, None] * residual


def body(flow, grid_velocity, cell_volume):
    inst_count = lax.axis_size("inst")
    own_index = lax.axis_index("inst")
    packed = jnp.concatenate([flow, grid_velocity], axis=1)
    extended = extended_2(packed, (("space", 2),), 1)
    ext_state = extended[:, :5]
    ext_grid = extended[:, 5:]
    slices = lax.all_gather(flow, "inst", axis=0, tiled=True)
    positions = jnp.arange(slices.shape[0], dtype=jnp.int32)
    weights = coefficient((own_index - positions) % inst_count, inst_count)
    added = jnp.einsum("j,jvxy->vxy", weights, slices, precision=lax.Precision.HIGHEST)
    derivative = added[None]
    summed = jnp.sum(slices, axis=0, keepdims=True)
    slab_width = flow.shape[3] // inst_count
    mean_flow = (
        lax.dynamic_slice_in_dim(summed[0], own_index * slab_width, slab_width, 2) / inst_count
    )
    flow_next = section_update(flow, grid_velocity, cell_volume, ext_state, ext_grid, derivative)
    return (flow_next, mean_flow)


LANES = 128
PIECES = 2


def spectral_weight(offset, count):
    if offset == 0:
        return 0.0
    angle = math.pi * offset / count
    return (-1.0) ** offset * (math.pi / count) * math.cos(angle) / math.sin(angle)


def cell_terms(state):
    inverse = 1.0 / state[0]
    speeds = [state[k] * inverse for k in (1, 2, 3)]
    kinetic = 0.5 * (state[1] * speeds[0] + state[2] * speeds[1] + state[3] * speeds[2])
    pressure = (gamma_ratio - 1.0) * (state[4] - kinetic)
    sound = jnp.sqrt(gamma_ratio * pressure * inverse)
    return speeds[0], speeds[1], pressure, sound


def rusanov(left, right, normal):
    state_l, speed_l, pressure_l, sound_l, grid_l = left
    state_r, speed_r, pressure_r, sound_r, grid_r = right
    face_speed = 0.5 * (grid_l + grid_r)
    relative_l = speed_l - face_speed
    relative_r = speed_r - face_speed
    reach = jnp.maximum(jnp.abs(relative_l) + sound_l, jnp.abs(relative_r) + sound_r)
    weight_l = 0.5 * (relative_l + reach)
    weight_r = 0.5 * (relative_r - reach)
    flux = [a * weight_l + b * weight_r for a, b in zip(state_l, state_r)]
    flux[1 + normal] += 0.5 * (pressure_l + pressure_r)
    flux[4] += 0.5 * (pressure_l * speed_l + pressure_r * speed_r)
    return flux


def on_side(change, side):
    return ([change(x) for x in side[0]],) + tuple(change(x) for x in side[1:])


def section_kernel(
    n,
    flow_hbm,
    grid_hbm,
    volume_hbm,
    next_ref,
    mean_ref,
    flow_ref,
    grid_ref,
    volume_ref,
    slabs,
    rates,
    returned,
    step_ref,
    edge_out,
    edge_in,
    edge_send,
    edge_recv,
    slab_send,
    slab_recv,
    rate_send,
    rate_recv,
    load_sem,
):
    variables, rows, columns = flow_ref.shape
    width = columns // n
    me = lax.axis_index("inst")
    other = 1 - lax.axis_index("space")
    order = sorted(range(1, n), key=lambda s: abs(2 * s - n))

    def peer(offset):
        return lax.rem(me + (offset + n), n)

    def columns_of(offset):
        return pl.ds(pl.multiple_of(peer(offset) * width, width), width)

    loads = [
        pltpu.make_async_copy(source, target, load_sem.at[k])
        for k, (source, target) in enumerate(
            ((flow_hbm, flow_ref), (grid_hbm, grid_ref), (volume_hbm, volume_ref))
        )
    ]
    for load in loads:
        load.start()
    barrier = pltpu.get_barrier_semaphore()
    for s in range(1, n):
        pl.semaphore_signal(barrier, inc=1, device_id={"inst": peer(s)})
    pl.semaphore_signal(barrier, inc=1, device_id={"space": other})
    loads[0].wait()
    pl.semaphore_wait(barrier, n)

    cuts = [-(-variables * k // PIECES) for k in range(PIECES + 1)]
    pieces = list(enumerate(slice(a, b) for a, b in zip(cuts, cuts[1:])))
    for k, c in pieces:
        for s in order:
            pltpu.make_async_remote_copy(
                src_ref=flow_ref.at[c, :, columns_of(s)],
                dst_ref=slabs.at[s - 1, c],
                send_sem=slab_send,
                recv_sem=slab_recv.at[k],
                device_id={"inst": peer(s)},
            ).start()

    for load in loads[1:]:
        load.wait()
    for edge, row in ((0, rows - 1), (1, 0)):
        for v in range(variables):
            edge_out[edge, v : v + 1, :] = flow_ref[v, row : row + 1, :]
        for v in range(2):
            edge_out[edge, variables + v : variables + v + 1, :] = grid_ref[v, row : row + 1, :]
        edge_out[edge, variables + 2 : variables + 3, :] = jnp.zeros((1, columns), jnp.float32)

    edges = pltpu.make_async_remote_copy(
        src_ref=edge_out,
        dst_ref=edge_in,
        send_sem=edge_send,
        recv_sem=edge_recv,
        device_id={"space": other},
    )
    edges.start()
    state = [flow_ref[v] for v in range(variables)]
    grid_0, grid_1, volume = grid_ref[0], grid_ref[1], volume_ref[...]
    speed_0, speed_1, pressure, sound = cell_terms(state)
    wave = jnp.abs(speed_0 - grid_0) + jnp.abs(speed_1 - grid_1) + 2.0 * sound
    push = (section_weight * courant_number) / (wave + math.pi * volume)
    step_ref[...] = push * volume

    lane = lax.broadcasted_iota(jnp.int32, (rows, columns), 1)
    own = (state, speed_1, pressure, sound, grid_1)
    left = on_side(lambda x: jnp.where(lane == 0, x, pltpu.roll(x, 1, 1)), own)
    flux = rusanov(left, own, 1)
    end = on_side(lambda x: x[:, columns - LANES :], own)
    last = rusanov(end, end, 1)
    lane_end = lane[:, columns - LANES :]
    for v in range(variables):
        upper = pltpu.roll(flux[v], columns - 1, 1)
        upper_end = jnp.where(lane_end == columns - 1, last[v], upper[:, columns - LANES :])
        upper = jnp.concatenate([upper[:, : columns - LANES], upper_end], axis=1)
        next_ref[v] = state[v] - push * (upper - flux[v])

    edges.wait_recv()

    def edge_side(edge):
        edge_state = [edge_in[edge, v : v + 1, :] for v in range(variables)]
        speed, _, edge_pressure, edge_sound = cell_terms(edge_state)
        grid = edge_in[edge, variables : variables + 1, :]
        return (edge_state, speed, edge_pressure, edge_sound, grid)

    above, below = edge_side(0), edge_side(1)
    row = lax.broadcasted_iota(jnp.int32, (rows, columns), 0)
    own = (state, speed_0, pressure, sound, grid_0)
    rolled = on_side(lambda x: pltpu.roll(x, 1, 0), own)
    first = lambda x, y: jnp.where(row == 0, y, x)
    left = (
        [first(x, y) for x, y in zip(rolled[0], above[0])],
    ) + tuple(first(x, y) for x, y in zip(rolled[1:], above[1:]))
    flux = rusanov(left, own, 0)
    last = rusanov(on_side(lambda x: x[rows - 1 : rows], own), below, 0)
    for v in range(variables):
        upper = jnp.where(row == rows - 1, last[v], pltpu.roll(flux[v], rows - 1, 0))
        next_ref[v] = next_ref[v] - push * (upper - flux[v])

    for k, c in pieces:
        got = slabs.at[:, c]
        pltpu.make_async_remote_copy(
            src_ref=got,
            dst_ref=got,
            send_sem=slab_send,
            recv_sem=slab_recv.at[k],
            device_id={"inst": peer(1)},
        ).wait_recv()
        held = [flow_ref[c, :, columns_of(0)]] + [slabs[s - 1, c] for s in range(1, n)]
        mean_ref[c] = functools.reduce(jnp.add, held) * (1.0 / n)

        def rate(t):
            terms = [held[s] * spectral_weight((s - t) % n, n) for s in range(n) if s != t]
            return functools.reduce(jnp.add, terms)

        for t in order:
            rates[t - 1, c] = rate(t)
            pltpu.make_async_remote_copy(
                src_ref=rates.at[t - 1, c],
                dst_ref=returned.at[t - 1, c],
                send_sem=rate_send,
                recv_sem=rate_recv.at[k],
                device_id={"inst": peer(-t)},
            ).start()
        at = columns_of(0)
        next_ref[c, :, at] = next_ref[c, :, at] - step_ref[:, at] * rate(0)

    for k, c in pieces:
        got = returned.at[:, c]
        pltpu.make_async_remote_copy(
            src_ref=got,
            dst_ref=got,
            send_sem=rate_send,
            recv_sem=rate_recv.at[k],
            device_id={"inst": peer(1)},
        ).wait_recv()
        for t in range(1, n):
            at = columns_of(t)
            next_ref[c, :, at] = next_ref[c, :, at] - step_ref[:, at] * returned[t - 1, c]

    edges.wait_send()
    for sent, sem in ((slabs, slab_send), (rates, rate_send)):
        pltpu.make_async_remote_copy(
            src_ref=sent,
            dst_ref=sent,
            send_sem=sem,
            recv_sem=edge_recv,
            device_id={"inst": peer(1)},
        ).wait_send()


def write_kernel(next_ref, mean_ref, next_hbm, mean_hbm, sems):
    writes = [
        pltpu.make_async_copy(next_ref, next_hbm, sems.at[0]),
        pltpu.make_async_copy(mean_ref, mean_hbm, sems.at[1]),
    ]
    for write in writes:
        write.start()
    for write in writes:
        write.wait()


def kernel_body(flow, grid_velocity, cell_volume):
    n = lax.axis_size("inst")
    variables, rows, columns = flow.shape[1:]
    width = columns // n
    f32 = jnp.float32
    exchanged = pltpu.VMEM((n - 1, variables, rows, width), f32)
    edge = pltpu.VMEM((2, variables + 3, columns), f32)
    dma = pltpu.SemaphoreType.DMA
    flow_next, mean_flow = pl.pallas_call(
        functools.partial(section_kernel, n),
        out_shape=(
            pltpu.VMEM((variables, rows, columns), f32),
            pltpu.VMEM((variables, rows, width), f32),
        ),
        in_specs=[pl.BlockSpec(memory_space=pltpu.HBM)] * 3,
        out_specs=[pl.BlockSpec(memory_space=pltpu.VMEM)] * 2,
        scratch_shapes=[
            pltpu.VMEM((variables, rows, columns), f32),
            pltpu.VMEM((2, rows, columns), f32),
            pltpu.VMEM((rows, columns), f32),
            exchanged,
            exchanged,
            exchanged,
            pltpu.VMEM((rows, columns), f32),
            edge,
            edge,
            dma,
            dma,
            dma,
            dma((PIECES,)),
            dma,
            dma((PIECES,)),
            dma((3,)),
        ],
        compiler_params=pltpu.CompilerParams(
            collective_id=0, has_side_effects=True, vmem_limit_bytes=32 * 1024 * 1024
        ),
        name="section",
    )(*[pltpu.with_memory_space_constraint(x, pltpu.HBM) for x in (flow[0], grid_velocity[0], cell_volume)])
    flow_next, mean_flow = pl.pallas_call(
        write_kernel,
        out_shape=(
            jax.ShapeDtypeStruct(flow_next.shape, f32),
            jax.ShapeDtypeStruct(mean_flow.shape, f32),
        ),
        in_specs=[pl.BlockSpec(memory_space=pltpu.VMEM)] * 2,
        out_specs=[pl.BlockSpec(memory_space=pltpu.HBM)] * 2,
        scratch_shapes=[dma((2,))],
        name="write",
    )(*[pltpu.with_memory_space_constraint(x, pltpu.VMEM) for x in (flow_next, mean_flow)])
    return flow_next[None], mean_flow


def solution(mesh):
    in_specs = (
        P(("groups", "inst"), None, "space", None),
        P(("groups", "inst"), None, "space", None),
        P("space", None),
    )
    out_specs = (P(("groups", "inst"), None, "space", None), P("groups", "space", "inst"))

    def local(flow, grid_velocity, cell_volume):
        whole_lanes = flow.shape[3] % (LANES * mesh.shape["inst"]) == 0
        whole_rows = flow.shape[2] % 8 == 0 and flow.shape[2] >= 8
        fits = mesh.shape["space"] == 2 and mesh.shape["inst"] > 1 and flow.shape[0] == 1
        chosen = kernel_body if whole_lanes and whole_rows and fits else body
        return chosen(flow, grid_velocity, cell_volume)

    return jax.shard_map(local, mesh=mesh, in_specs=in_specs, out_specs=out_specs, check_vma=False)
```
